32 devices in a mesh: parts: 2 (over y), blk: 4 (over z), lay: 4 (over x, core).
Axes of the slice: x: 2, y: 2, z: 4, core: 2. Of those that a mesh axis runs over, the one named last changes fastest.
Arguments:
- query_grads: bfloat16 [1024, 4, 4096], P(('parts', 'blk'), 'lay'), parts along dimension 0, may hold values from -6 to 6
- train_grads: bfloat16 [2048, 4, 4096], P(('parts', 'blk'), 'lay'), parts along dimension 0, may hold values from -6 to 6
- basis_out: float32 [4, 64, 64], P('lay'), may hold values from -0.75 to 0.75
- basis_in: float32 [4, 64, 64], P('lay'), may hold values from -0.75 to 0.75
- spectrum: float32 [4, 4096], P('lay'), may hold values from 0.3 to 10
- train_ids: int32 [8, 256], P(('parts', 'blk')), parts along dimension 0, may hold values from 0 to 255, each once within a row
Outputs:
- scores: float32 [1024, 1024], P(('parts', 'lay'), 'blk'), parts along dimension 0
The draws below stay inside these ranges and needn't reach their ends.
There are 2 independent parts, one for each index of `parts`. The reference program is written for one: setup_inputs(seed, part) draws one part's arguments, and reference() takes and returns one part's arrays. A program takes and returns all parts, laid end to end along the dimension named above; an argument that names none is the same for every part. Nothing has to cross between parts.
Inputs may be any that keep to these rules, and one draw needn't show every extreme that they name: Each row of train_ids holds every number of 0 to 255 once.
All inputs are finite; a program needn't handle non-finite values.
Results may differ from the reference program's by a relative error of at most 0.0029.
Values may be sent and summed in bfloat16 or wider, within the bound.
A program may use at most 128 MiB of HBM per device.

```python
import math
import jax
import jax.numpy as jnp
from jax import lax

PROJ_OUT = 64
PROJ_IN = 64
ROWS_DEV = 256
LAYERS = 4
QUERIES = 512
TRAIN = 1024
N_BLK = 4


def levels(rng, dims, shards, smallest, largest):
    loudness, own = 1.0, jax.random.fold_in(rng, 6)
    for dim, shards_of in shards:
        draws = jnp.exp(jax.random.uniform(jax.random.fold_in(own, dim), (shards_of,), jnp.float32, smallest / len(shards), largest / len(shards)))
        loudness = loudness * jnp.repeat(draws, dims[dim] // shards_of).reshape([-1 if axis == dim else 1 for axis in range(len(dims))])
    return loudness


def normal_values(key, extent, spread, limit, cuts=(), held_as=jnp.bfloat16):
    drawn = spread * jax.random.normal(key, extent, jnp.float32)
    if cuts:
        drawn = drawn * levels(key, extent, cuts, -0.22, 0.18)
    return jnp.clip(drawn, -limit, limit).astype(held_as)


def setup_inputs(seed: int = 0, part: int = 0) -> dict:
    streams_of = jax.random.split(jax.random.key(seed), 7)
    part_splits = jax.random.split(jax.random.fold_in(streams_of[6], part), 7)
    return {
        "query_grads": normal_values(part_splits[0], (QUERIES, LAYERS, PROJ_OUT * PROJ_IN), 1.0, 6.0, ((0, 4), (1, 4))),
        "train_grads": normal_values(part_splits[1], (TRAIN, LAYERS, PROJ_OUT * PROJ_IN), 1.0, 6.0, ((0, 4), (1, 4))),
        "basis_out": normal_values(streams_of[2], (LAYERS, PROJ_OUT, PROJ_OUT), PROJ_OUT ** -0.5, 0.75, ((0, 4),), jnp.float32),
        "basis_in": normal_values(streams_of[3], (LAYERS, PROJ_IN, PROJ_IN), PROJ_IN ** -0.5, 0.75, ((0, 4),), jnp.float32),
        "spectrum": jnp.clip(jnp.exp(math.log(10.0) - 3.506558 * jax.random.uniform(streams_of[4], (LAYERS, PROJ_OUT * PROJ_IN), jnp.float32) ** levels(streams_of[4], (LAYERS, PROJ_OUT * PROJ_IN), ((0, 4),), -0.2, 0.2)), 0.3, 10.0),
        "train_ids": jax.vmap(lambda own: jax.random.permutation(own, ROWS_DEV))(jax.random.split(part_splits[5], N_BLK)).reshape((N_BLK, ROWS_DEV)).astype(jnp.int32),
    }


damping = 0.1
score_scale = 1.0 / 256.0


def precondition(grads, basis_out, basis_in, spectrum):
    row_count = grads.shape[0]
    lay_count = grads.shape[1]
    out_dim = basis_out.shape[1]
    in_dim = basis_in.shape[1]
    field = grads.astype(jnp.float32).reshape(row_count, lay_count, out_dim, in_dim)
    high = lax.Precision.HIGHEST
    rotated = jnp.einsum("lap,mlab->mlpb", basis_out, field, precision=high)
    rotated = jnp.einsum("mlpb,lbr->mlpr", rotated, basis_in, precision=high)
    scaled = rotated / (spectrum.reshape(1, lay_count, out_dim, in_dim) + damping)
    restored = jnp.einsum("lap,mlpr->mlar", basis_out, scaled, precision=high)
    restored = jnp.einsum("mlar,lbr->mlab", restored, basis_in, precision=high)
    return restored.reshape(row_count, lay_count * out_dim * in_dim).astype(jnp.bfloat16)


def reference(query_grads, train_grads, basis_out, basis_in, spectrum, train_ids):
    prepared = precondition(query_grads, basis_out, basis_in, spectrum)
    flat_train = train_grads.reshape(train_grads.shape[0], -1)
    raw = lax.dot_general(prepared, flat_train, (((1,), (1,)), ((), ())), preferred_element_type=jnp.float32)
    raw = raw * score_scale
    columns = (jnp.arange(N_BLK, dtype=jnp.int32)[:, None] * ROWS_DEV + train_ids.astype(jnp.int32)).reshape(-1)
    return jnp.take(raw, columns, axis=1)
```

```python
import functools

import jax
import jax.numpy as jnp
from jax import lax
from jax.experimental import pallas as pl
from jax.experimental.pallas import tpu as pltpu
from jax.sharding import PartitionSpec as P

damping = 0.1
score_scale = 1.0 / 256.0
MESH = pl.DeviceIdType.MESH
f32 = jnp.float32
bf16 = jnp.bfloat16


def precondition(grads, basis_out, basis_in, spectrum):
    row_count = grads.shape[0]
    lay_count = grads.shape[1]
    out_dim = basis_out.shape[1]
    in_dim = basis_in.shape[1]
    field = grads.astype(jnp.float32).reshape(row_count, lay_count, out_dim, in_dim)
    high = lax.Precision.HIGHEST
    rotated = jnp.einsum("lap,mlab->mlpb", basis_out, field, precision=high)
    rotated = jnp.einsum("mlpb,lbr->mlpr", rotated, basis_in, precision=high)
    scaled = rotated / (spectrum.reshape(1, lay_count, out_dim, in_dim) + damping)
    restored = jnp.einsum("lap,mlpr->mlar", basis_out, scaled, precision=high)
    restored = jnp.einsum("mlar,lbr->mlab", restored, basis_in, precision=high)
    return restored.reshape(row_count, lay_count * out_dim * in_dim).astype(jnp.bfloat16)


def plain(query_grads, train_grads, basis_out, basis_in, spectrum, train_ids):
    prepared = precondition(query_grads, basis_out, basis_in, spectrum)
    local_rows = train_grads.reshape(train_grads.shape[0], -1)
    all_queries = lax.all_gather(prepared, "blk", axis=0, tiled=True)
    summed = lax.psum_scatter(
        lax.dot_general(
            all_queries, local_rows, (((1,), (1,)), ((), ())), preferred_element_type=jnp.float32
        ),
        "lay",
        scatter_dimension=0,
        tiled=True,
    )
    scaled_scores = summed * score_scale
    return jnp.take(scaled_scores, train_ids[0], axis=1)


def dot(a, b, dims=((1,), (0,))):
    return lax.dot_general(a, b, (dims, ((), ())), preferred_element_type=f32)


def split(x):
    hi = x.astype(bf16)
    return hi, (x - hi.astype(f32)).astype(bf16)


def dot3(a_hi, a_lo, b):
    b_hi, b_lo = split(b)
    return dot(a_hi, b_hi) + (dot(a_hi, b_lo) + dot(a_lo, b_hi))


CH = 16
GR = 64
SIDE = 64
TILE = 256


def kernel(n, q_hbm, t_hbm, bo_ref, bi_ref, sp_ref, ids_ref, o_ref,
           q_all, t_ref, x_ref, tp_hi, tp_lo, perm, diag, stage, red,
           load_sem, send_sem, recv_sem, rsend_sem, rrecv_sem):
    z = lax.axis_index("blk")
    l = lax.axis_index("lay")
    rows = q_hbm.shape[0]
    cols = t_ref.shape[0]
    width = q_hbm.shape[1]
    tiles = width // TILE
    C = rows // CH
    G = rows // GR
    T = (n - 1) * C

    own = pltpu.make_async_copy(
        q_hbm, q_all.at[pl.ds(pl.multiple_of(z * rows, rows), rows), :], load_sem.at[0])
    own.start()
    train = pltpu.make_async_copy(t_hbm, t_ref, load_sem.at[1])
    train.start()

    barrier = pltpu.get_barrier_semaphore()

    @pl.when(z > 0)
    def _():
        pl.semaphore_signal(barrier, inc=1, device_id={"blk": z - 1}, device_id_type=MESH)

    @pl.when(z < n - 1)
    def _():
        pl.semaphore_signal(barrier, inc=1, device_id={"blk": z + 1}, device_id_type=MESH)

    for k in range(1, n):
        pl.semaphore_signal(
            barrier, inc=1, device_id={"lay": lax.rem(l + k, n)}, device_id_type=MESH)

    row_i = lax.broadcasted_iota(jnp.int32, (TILE, SIDE), 0)
    col_i = lax.broadcasted_iota(jnp.int32, (TILE, SIDE), 1)
    pick = jnp.where(lax.rem(row_i, SIDE) == col_i, 1.0, 0.0).astype(bf16)
    big_r = lax.broadcasted_iota(jnp.int32, (TILE, TILE), 0)
    big_c = lax.broadcasted_iota(jnp.int32, (TILE, TILE), 1)
    same = big_r // SIDE == big_c // SIDE

    def spread(base, side):
        half = dot(pick, base, ((1,), (side,))).astype(bf16)
        full = dot(half, pick, ((1,), (1,)))
        return jnp.where(same, full, 0.0).astype(bf16)

    for k, (ref, side) in enumerate(((bi_ref, 1), (bo_ref, 1), (bo_ref, 0), (bi_ref, 0))):
        hi, lo = split(ref[...])
        diag[2 * k] = spread(hi, side)
        diag[2 * k + 1] = spread(lo, side)
    perm[...] = jnp.where(big_r == ids_ref[...], 1.0, 0.0).astype(bf16)

    own.wait()
    train.wait()
    pl.semaphore_wait(
        barrier, (n - 1) + (z > 0).astype(jnp.int32) + (z < n - 1).astype(jnp.int32))

    def chunk(block, c):
        return q_all.at[pl.ds(pl.multiple_of(block * rows + c * CH, CH), CH), :]

    def copy(way, t, block, target):
        part = chunk(block, lax.rem(t, C))
        return pltpu.make_async_remote_copy(
            src_ref=part, dst_ref=part, send_sem=send_sem.at[way, t],
            recv_sem=recv_sem.at[way, t], device_id={"blk": target}, device_id_type=MESH)

    def send_right(t):
        return copy(0, t, z - t // C, z + 1)

    def send_left(t):
        return copy(1, t, z + t // C, z - 1)

    def from_left(t):
        return copy(0, t, z - 1 - t // C, z + 1)

    def from_right(t):
        return copy(1, t, z + 1 + t // C, z - 1)

    def goes_right(t):
        return (t >= 0) & (t < T) & (z < n - 1) & (t // C <= z)

    def goes_left(t):
        return (t >= 0) & (t < T) & (z > 0) & (z + t // C <= n - 1)

    def comes_left(t):
        return (t >= 0) & (t < T) & (z - 1 - t // C >= 0)

    def comes_right(t):
        return (t >= 0) & (t < T) & (z + 1 + t // C <= n - 1)

    def reduce_copy(block, g):
        return pltpu.make_async_remote_copy(
            src_ref=stage.at[block, pl.ds(pl.multiple_of(g * GR, GR), GR), :],
            dst_ref=red.at[l, pl.ds(pl.multiple_of(g * GR, GR), GR), :],
            send_sem=rsend_sem.at[block, g], recv_sem=rrecv_sem.at[l, g],
            device_id={"lay": block}, device_id_type=MESH)

    def scores(block, g, count):
        first = pl.multiple_of(block * rows + g * GR, GR)
        part = q_all[pl.ds(first, count * GR), :]
        total = dot(part, tp_hi[...]) + dot(part, tp_lo[...])

        @pl.when(block == l)
        def _():
            red[l, pl.ds(pl.multiple_of(g * GR, GR), count * GR), :] = total

        @pl.when(block != l)
        def _():
            stage[block, pl.ds(pl.multiple_of(g * GR, GR), count * GR), :] = total
            for k in range(count):
                reduce_copy(block, g + k).start()

    def turn_in(i, carry):
        at = pl.multiple_of(i * TILE, TILE)
        x = dot(t_ref[:, pl.ds(at, TILE)], perm[...], ((0,), (0,))).astype(bf16)
        x = dot(diag[0], x) + dot(diag[1], x)
        for h in range(cols // 128):
            x_ref[h, pl.ds(at, TILE), :] = x[:, h * 128:(h + 1) * 128]
        return carry

    group = TILE // SIDE

    def turn_out(i, carry):
        halves = []
        for h in range(cols // 128):
            halves.append(jnp.concatenate(
                [x_ref[h, pl.ds(i * group + k, SIDE, stride=SIDE), :] for k in range(group)], axis=0))
        x = jnp.concatenate(halves, axis=1)
        x = dot3(diag[2], diag[3], x)
        lane = lax.broadcasted_iota(jnp.int32, (TILE, SIDE), 1)
        which = lax.broadcasted_iota(jnp.int32, (TILE, SIDE), 0) // SIDE + i * group
        values = jnp.concatenate([sp_ref[...]] * group, axis=0)
        column = jnp.sum(jnp.where(lane == which, values, 0.0), axis=1, keepdims=True)
        x = x * (1.0 / (column + damping))
        x = dot3(diag[4], diag[5], x)
        for h in range(cols // 128):
            for k in range(group):
                x_ref[h, pl.ds(i * group + k, SIDE, stride=SIDE), :] = (
                    x[k * SIDE:(k + 1) * SIDE, h * 128:(h + 1) * 128])
        return carry

    def turn_back(i, carry):
        at = pl.multiple_of(i * TILE, TILE)
        x = jnp.concatenate(
            [x_ref[h, pl.ds(at, TILE), :] for h in range(cols // 128)], axis=1)
        hi, lo = split(dot3(diag[6], diag[7], x))
        tp_hi[pl.ds(at, TILE), :] = hi
        tp_lo[pl.ds(at, TILE), :] = lo
        return carry

    def step(t, carry):
        for goes, send in ((goes_right, send_right), (goes_left, send_left)):
            @pl.when(goes(t - 2))
            def _():
                send(t - 2).wait_send()

            @pl.when(goes(t))
            def _():
                send(t).start()

        @pl.when(t < 2)
        def _():
            lax.fori_loop(t * (tiles // 2), (t + 1) * (tiles // 2), turn_in, 0)

        @pl.when((t >= 2) & (t < 6))
        def _():
            lax.fori_loop((t - 2) * (tiles // 4), (t - 1) * (tiles // 4), turn_out, 0)

        @pl.when((t >= 6) & (t < 8))
        def _():
            lax.fori_loop((t - 6) * (tiles // 2), (t - 5) * (tiles // 2), turn_back, 0)

        r = t - 1
        for comes, got in ((comes_left, from_left), (comes_right, from_right)):
            @pl.when(comes(r))
            def _():
                got(r).wait_recv()

        early = jnp.where(t == C, z, jnp.where(t == C + 1, z - 1, z + 1))

        @pl.when((t >= C) & (t <= C + 2) & (early >= 0) & (early < n))
        def _():
            scores(early, 0, G)

        last = lax.rem(r, GR // CH) == GR // CH - 1
        for comes, sign in ((comes_left, -1), (comes_right, 1)):
            @pl.when((r >= C) & last & comes(r))
            def _():
                scores(z + sign * (1 + r // C), lax.rem(r, C) // (GR // CH), 1)
        return carry

    lax.fori_loop(0, T + 2, step, 0)

    for k in range(1, n):
        other = lax.rem(l + k, n)
        for g in range(G):
            reduce_copy(other, g).wait_send()
            pltpu.make_async_remote_copy(
                src_ref=stage.at[other, pl.ds(g * GR, GR), :],
                dst_ref=red.at[other, pl.ds(g * GR, GR), :],
                send_sem=rsend_sem.at[other, g], recv_sem=rrecv_sem.at[other, g],
                device_id={"lay": other}, device_id_type=MESH).wait_recv()
    total = red[0]
    for k in range(1, n):
        total = total + red[k]
    o_ref[...] = total * score_scale


def per_device(n, query_grads, train_grads, basis_out, basis_in, spectrum, train_ids):
    rows, lay_count, width = query_grads.shape
    cols = train_grads.shape[0]
    C = rows // CH
    T = (n - 1) * C
    vmem = pl.BlockSpec(memory_space=pltpu.VMEM)
    hbm = pl.BlockSpec(memory_space=pl.ANY)
    return pl.pallas_call(
        functools.partial(kernel, n),
        out_shape=jax.ShapeDtypeStruct((rows, cols), f32),
        in_specs=[hbm, hbm, vmem, vmem, vmem, vmem],
        out_specs=vmem,
        scratch_shapes=[
            pltpu.VMEM((n * rows, width), bf16),
            pltpu.VMEM((cols, width), bf16),
            pltpu.VMEM((cols // 128, width, 128), f32),
            pltpu.VMEM((width, cols), bf16),
            pltpu.VMEM((width, cols), bf16),
            pltpu.VMEM((cols, cols), bf16),
            pltpu.VMEM((8, TILE, TILE), bf16),
            pltpu.VMEM((n, rows, cols), f32),
            pltpu.VMEM((n, rows, cols), f32),
            pltpu.SemaphoreType.DMA((2,)),
            pltpu.SemaphoreType.DMA((2, T)),
            pltpu.SemaphoreType.DMA((2, T)),
            pltpu.SemaphoreType.DMA((n, rows // GR)),
            pltpu.SemaphoreType.DMA((n, rows // GR)),
        ],
        compiler_params=pltpu.CompilerParams(
            collective_id=0, has_side_effects=True, vmem_limit_bytes=48 * 1024 * 1024),
    )(
        query_grads.reshape(rows, width),
        train_grads.reshape(cols, width),
        basis_out.reshape(SIDE, SIDE),
        basis_in.reshape(SIDE, SIDE),
        spectrum.reshape(SIDE, SIDE),
        train_ids,
    )


def solution(mesh):
    in_specs = (
        P(("parts", "blk"), "lay", None),
        P(("parts", "blk"), "lay", None),
        P("lay", None, None),
        P("lay", None, None),
        P("lay", None),
        P(("parts", "blk"), None),
    )
    out_specs = P(("parts", "lay"), "blk")
    n = mesh.shape["blk"]
    body = functools.partial(per_device, n) if n == mesh.shape["lay"] else plain
    return jax.shard_map(body, mesh=mesh, in_specs=in_specs, out_specs=out_specs, check_vma=False)
```

```python
import functools

import jax
import jax.numpy as jnp
from jax import lax
from jax.experimental import pallas as pl
from jax.experimental.pallas import tpu as pltpu
from jax.sharding import PartitionSpec as P

damping = 0.1
score_scale = 1.0 / 256.0
MESH = pl.DeviceIdType.MESH
f32 = jnp.float32
bf16 = jnp.bfloat16


def precondition(grads, basis_out, basis_in, spectrum):
    row_count = grads.shape[0]
    lay_count = grads.shape[1]
    out_dim = basis_out.shape[1]
    in_dim = basis_in.shape[1]
    field = grads.astype(jnp.float32).reshape(row_count, lay_count, out_dim, in_dim)
    high = lax.Precision.HIGHEST
    rotated = jnp.einsum("lap,mlab->mlpb", basis_out, field, precision=high)
    rotated = jnp.einsum("mlpb,lbr->mlpr", rotated, basis_in, precision=high)
    scaled = rotated / (spectrum.reshape(1, lay_count, out_dim, in_dim) + damping)
    restored = jnp.einsum("lap,mlpr->mlar", basis_out, scaled, precision=high)
    restored = jnp.einsum("mlar,lbr->mlab", restored, basis_in, precision=high)
    return restored.reshape(row_count, lay_count * out_dim * in_dim).astype(jnp.bfloat16)


def plain(query_grads, train_grads, basis_out, basis_in, spectrum, train_ids):
    prepared = precondition(query_grads, basis_out, basis_in, spectrum)
    local_rows = train_grads.reshape(train_grads.shape[0], -1)
    all_queries = lax.all_gather(prepared, "blk", axis=0, tiled=True)
    summed = lax.psum_scatter(
        lax.dot_general(
            all_queries, local_rows, (((1,), (1,)), ((), ())), preferred_element_type=jnp.float32
        ),
        "lay",
        scatter_dimension=0,
        tiled=True,
    )
    scaled_scores = summed * score_scale
    return jnp.take(scaled_scores, train_ids[0], axis=1)


def dot(a, b, dims=((1,), (0,))):
    return lax.dot_general(a, b, (dims, ((), ())), preferred_element_type=f32)


def split(x):
    hi = x.astype(bf16)
    return hi, (x - hi.astype(f32)).astype(bf16)


def dot3(a_hi, a_lo, b):
    b_hi, b_lo = split(b)
    return dot(a_hi, b_hi) + (dot(a_hi, b_lo) + dot(a_lo, b_hi))


CH = 16
GR = 64
SIDE = 64
TILE = 256
MOVED = 7


def kernel(n, q_hbm, t_hbm, bo_hbm, bi_hbm, sp_hbm, ids_hbm, o_ref,
           q_all, t_ref, bo_ref, bi_ref, sp_ref, ids_ref, sq_ref,
           x_ref, tp_hi, tp_lo, tp_end, perm, diag, stage, red, estage, ered,
           load_sem, a_send, a_recv, b_send, b_recv, c_send, c_recv,
           e_send, e_recv, r_send, r_recv):
    z = lax.axis_index("blk")
    l = lax.axis_index("lay")
    rows = q_hbm.shape[0]
    cols = t_ref.shape[0]
    width = q_hbm.shape[1]
    tiles = width // TILE
    C = rows // CH
    G = rows // GR
    KF = MOVED * TILE
    low = z < n // 2
    end = jnp.where(low, 0, n - 1)
    mid = jnp.where(low, 1, n - 2)
    far_mid = n - 1 - mid
    far_end = n - 1 - end
    at_end = z == end
    at_mid = z == mid

    def place(block, row, count, unit):
        return pl.ds(pl.multiple_of(block * rows + row, unit), count)

    loads = [
        pltpu.make_async_copy(q_hbm, q_all.at[place(z, 0, rows, rows), :], load_sem.at[0]),
        pltpu.make_async_copy(bo_hbm, bo_ref, load_sem.at[1]),
        pltpu.make_async_copy(bi_hbm, bi_ref, load_sem.at[2]),
        pltpu.make_async_copy(sp_hbm, sp_ref, load_sem.at[3]),
        pltpu.make_async_copy(ids_hbm, ids_ref, load_sem.at[4]),
        pltpu.make_async_copy(t_hbm, t_ref, load_sem.at[5]),
    ]
    for load in loads:
        load.start()

    barrier = pltpu.get_barrier_semaphore()
    partner = jnp.where(at_end, mid, end)
    for k in range(n):
        pl.semaphore_signal(
            barrier, inc=1, device_id={"blk": partner, "lay": k}, device_id_type=MESH)
    for k in range(1, n):
        pl.semaphore_signal(
            barrier, inc=1, device_id={"lay": lax.rem(l + k, n)}, device_id_type=MESH)

    @pl.when(at_mid)
    def _():
        pl.semaphore_signal(barrier, inc=1, device_id={"blk": far_mid}, device_id_type=MESH)

    def remote(src, dst, send, recv, target):
        return pltpu.make_async_remote_copy(
            src_ref=src, dst_ref=dst, send_sem=send, recv_sem=recv,
            device_id=target, device_id_type=MESH)

    def a_query(t):
        part = q_all.at[place(end, t * CH, CH, CH), :]
        return remote(part, part, a_send.at[t], a_recv.at[t], {"blk": mid})

    def a_train(m):
        piece = pl.ds(pl.multiple_of(m * TILE, TILE), TILE)
        return remote(tp_hi.at[piece, :], tp_end.at[piece, :],
                      a_send.at[C + m], a_recv.at[C + m], {"blk": mid})

    def b_out(t):
        part = q_all.at[place(jnp.where(t < C, mid, end), lax.rem(t, C) * CH, CH, CH), :]
        return remote(part, part, b_send.at[t], b_recv.at[t], {"blk": far_mid})

    def b_in(t):
        part = q_all.at[place(jnp.where(t < C, far_mid, far_end), lax.rem(t, C) * CH, CH, CH), :]
        return remote(part, part, b_send.at[t], b_recv.at[t], {"blk": far_mid})

    def c_own(t):
        part = q_all.at[place(mid, t * CH, CH, CH), pl.ds(KF, width - KF)]
        return remote(part, part, c_send.at[t], c_recv.at[t], {"blk": end})

    def c_far(t):
        part = q_all.at[place(jnp.where(t < C, far_mid, far_end), lax.rem(t, C) * CH, CH, CH),
                        pl.ds(KF, width - KF)]
        return remote(part, part, c_send.at[C + t], c_recv.at[C + t], {"blk": end})

    def e_copy(block, g, sender):
        part = pl.ds(pl.multiple_of(g * GR, GR), GR)
        return remote(estage.at[block, part, :], ered.at[sender, part, :],
                      e_send.at[block, g], e_recv.at[sender, g], {"blk": end, "lay": block})

    def r_copy(block, g, sender):
        part = pl.ds(pl.multiple_of(g * GR, GR), GR)
        return remote(stage.at[block, part, :], red.at[sender, part, :],
                      r_send.at[block, g], r_recv.at[sender, g], {"lay": block})

    for load in loads[1:5]:
        load.wait()
    row_i = lax.broadcasted_iota(jnp.int32, (TILE, SIDE), 0)
    col_i = lax.broadcasted_iota(jnp.int32, (TILE, SIDE), 1)
    pick = jnp.where(lax.rem(row_i, SIDE) == col_i, 1.0, 0.0).astype(bf16)
    big_r = lax.broadcasted_iota(jnp.int32, (TILE, TILE), 0)
    big_c = lax.broadcasted_iota(jnp.int32, (TILE, TILE), 1)
    same = big_r // SIDE == big_c // SIDE
    group = TILE // SIDE

    def spread(base, side):
        half = dot(pick, base, ((1,), (side,))).astype(bf16)
        full = dot(half, pick, ((1,), (1,)))
        return jnp.where(same, full, 0.0).astype(bf16)

    def prepare():
        for k, (ref, side) in enumerate(((bi_ref, 1), (bo_ref, 1), (bo_ref, 0), (bi_ref, 0))):
            hi, lo = split(ref[0])
            diag[2 * k] = spread(hi, side)
            diag[2 * k + 1] = spread(lo, side)
        perm[...] = jnp.where(big_r == ids_ref[...], 1.0, 0.0).astype(bf16)
        for p in range(SIDE):
            sq_ref[p:p + 1, :] = 1.0 / (sp_ref[:, p * SIDE:(p + 1) * SIDE] + damping)

    loads[0].wait()
    loads[5].wait()
    pl.semaphore_wait(barrier, 2 * n - 1 + at_mid.astype(jnp.int32))

    def scores(block, g, count, first=0):
        here = place(block, g * GR, count * GR, GR)
        part = q_all[here, first:]
        total = dot(part, tp_hi[first:, :]) + dot(part, tp_lo[first:, :])
        span = pl.ds(pl.multiple_of(g * GR, GR), count * GR)

        @pl.when(block == l)
        def _():
            red[l, span, :] = total

        @pl.when(block != l)
        def _():
            stage[block, span, :] = total
            for k in range(count):
                r_copy(block, g + k, l).start()

    def moved_scores(block, g, count):
        part = q_all[place(block, g * GR, count * GR, GR), :KF]
        span = pl.ds(pl.multiple_of(g * GR, GR), count * GR)
        estage[block, span, :] = dot(part, tp_end[...]).astype(bf16)
        for k in range(count):
            e_copy(block, g + k, l).start()

    def turn_in(i, carry):
        at = pl.multiple_of(i * TILE, TILE)
        x = dot(t_ref[:, pl.ds(at, TILE)], perm[...], ((0,), (0,))).astype(bf16)
        x = dot(diag[0], x) + dot(diag[1], x)
        for h in range(cols // 128):
            x_ref[h, pl.ds(at, TILE), :] = x[:, h * 128:(h + 1) * 128]
        return carry

    def turn_out(i, carry):
        halves = []
        for h in range(cols // 128):
            halves.append(jnp.concatenate(
                [x_ref[h, pl.ds(i * group + k, SIDE, stride=SIDE), :] for k in range(group)], axis=0))
        x = jnp.concatenate(halves, axis=1)
        x = dot3(diag[2], diag[3], x)
        lane = lax.broadcasted_iota(jnp.int32, (TILE, SIDE), 1)
        which = lax.broadcasted_iota(jnp.int32, (TILE, SIDE), 0) // SIDE + i * group
        values = jnp.concatenate([sq_ref[...]] * group, axis=0)
        x = x * jnp.sum(jnp.where(lane == which, values, 0.0), axis=1, keepdims=True)
        x = dot3(diag[4], diag[5], x)
        for h in range(cols // 128):
            for k in range(group):
                x_ref[h, pl.ds(i * group + k, SIDE, stride=SIDE), :] = (
                    x[k * SIDE:(k + 1) * SIDE, h * 128:(h + 1) * 128])
        return carry

    def turn_back(i, carry):
        at = pl.multiple_of(i * TILE, TILE)
        x = jnp.concatenate(
            [x_ref[h, pl.ds(at, TILE), :] for h in range(cols // 128)], axis=1)
        hi, lo = split(dot3(diag[6], diag[7], x))
        tp_hi[pl.ds(at, TILE), :] = hi
        tp_lo[pl.ds(at, TILE), :] = lo
        return carry

    LAG = 3
    PER = GR // CH

    def when(*parts):
        test = parts[0]
        for part in parts[1:]:
            test = test & part
        return pl.when(test)

    def within(t, first, last):
        return (t >= first) & (t < last)

    def step(t, carry):
        @when(at_end, within(t - LAG, 0, C))
        def _():
            a_query(t - LAG).wait_send()

        @when(at_end, within(t - LAG, C, C + MOVED))
        def _():
            a_train(t - LAG - C).wait_send()

        @when(at_end, t < C)
        def _():
            a_query(t).start()

        @when(at_end, within(t, C, C + MOVED))
        def _():
            a_train(t - C).start()

        @when(at_mid, within(t - LAG, 0, 2 * C))
        def _():
            b_out(t - LAG).wait_send()

        @when(at_mid, t < 2 * C)
        def _():
            b_out(t).start()

        even = lax.rem(t, 2) == 0

        @when(at_mid, even, t < 2 * C)
        def _():
            c_own(t // 2).start()

        @pl.when(t == 0)
        def _():
            prepare()

        @pl.when(t < 2)
        def _():
            lax.fori_loop(t * (tiles // 2), (t + 1) * (tiles // 2), turn_in, 0)

        @pl.when(within(t, 2, 6))
        def _():
            lax.fori_loop((t - 2) * (tiles // 4), (t - 1) * (tiles // 4), turn_out, 0)

        @pl.when(within(t, 6, 8))
        def _():
            lax.fori_loop((t - 6) * (tiles // 2), (t - 5) * (tiles // 2), turn_back, 0)

        @when(at_mid, within(t - 1, 0, C))
        def _():
            a_query(t - 1).wait_recv()

        @when(at_mid, within(t - 1, C, C + MOVED))
        def _():
            a_train(t - 1 - C).wait_recv()

        @when(at_mid, within(t - 1, 0, 2 * C))
        def _():
            b_in(t - 1).wait_recv()
            c_far(t - 1).start()

        @when(at_end, within(t - 1, 0, 2 * C), ~even)
        def _():
            c_own((t - 1) // 2).wait_recv()

        @when(at_end, within(t - 2, 0, 2 * C))
        def _():
            c_far(t - 2).wait_recv()

        early = jnp.where(t == C, mid, jnp.where(t == C + 1, end, far_mid))

        @when(at_mid, within(t, C, C + 3))
        def _():
            scores(early, 0, G)

        @when(at_mid, within(t - 1, C, 2 * C), lax.rem(t - 1, PER) == PER - 1)
        def _():
            scores(far_end, lax.rem(t - 1, C) // PER, 1)

        @when(at_mid, t == C + MOVED)
        def _():
            moved_scores(mid, 0, G)
            moved_scores(far_mid, 0, G)
            moved_scores(far_end, 0, 1)

        @when(at_mid, t == 2 * C)
        def _():
            moved_scores(far_end, 1, 1)

        @when(at_end, t == C)
        def _():
            scores(end, 0, G)

        @when(at_end, t == C + 2)
        def _():
            scores(far_mid, 0, G, KF)

        @when(at_end, t == 2 * C)
        def _():
            scores(mid, 0, G, KF)

        @when(at_end, within(t - 2, C, 2 * C), lax.rem(t - 2, PER) == PER - 1)
        def _():
            scores(far_end, lax.rem(t - 2, C) // PER, 1, KF)
        return carry

    lax.fori_loop(0, 2 * C + LAG, step, 0)

    @pl.when(at_mid)
    def _():
        def sent(t, carry):
            c_far(t).wait_send()
            return carry

        def sent_own(t, carry):
            c_own(t).wait_send()
            return carry

        lax.fori_loop(0, 2 * C, sent, 0)
        lax.fori_loop(0, C, sent_own, 0)
        for block in (mid, far_mid, far_end):
            for g in range(G):
                e_copy(block, g, l).wait_send()

    for k in range(1, n):
        other = lax.rem(l + k, n)
        for g in range(G):
            r_copy(other, g, l).wait_send()
            r_copy(other, g, other).wait_recv()
    total = red[0]
    for k in range(1, n):
        total = total + red[k]
    o_ref[...] = total * score_scale

    @pl.when(at_end & (l != end))
    def _():
        for k in range(n):
            for g in range(G):
                e_copy(l, g, k).wait_recv()
        extra = ered[0].astype(f32)
        for k in range(1, n):
            extra = extra + ered[k].astype(f32)
        o_ref[...] += extra * score_scale


def per_device(n, query_grads, train_grads, basis_out, basis_in, spectrum, train_ids):
    rows, lay_count, width = query_grads.shape
    cols = train_grads.shape[0]
    C = rows // CH
    G = rows // GR
    hbm = pl.BlockSpec(memory_space=pl.ANY)
    dma = pltpu.SemaphoreType.DMA
    return pl.pallas_call(
        functools.partial(kernel, n),
        out_shape=jax.ShapeDtypeStruct((rows, cols), f32),
        in_specs=[hbm] * 6,
        out_specs=pl.BlockSpec(memory_space=pltpu.VMEM),
        scratch_shapes=[
            pltpu.VMEM((n * rows, width), bf16),
            pltpu.VMEM((cols, width), bf16),
            pltpu.VMEM((1, SIDE, SIDE), f32),
            pltpu.VMEM((1, SIDE, SIDE), f32),
            pltpu.VMEM((1, width), f32),
            pltpu.VMEM((1, cols), jnp.int32),
            pltpu.VMEM((SIDE, SIDE), f32),
            pltpu.VMEM((cols // 128, width, 128), f32),
            pltpu.VMEM((width, cols), bf16),
            pltpu.VMEM((width, cols), bf16),
            pltpu.VMEM((MOVED * TILE, cols), bf16),
            pltpu.VMEM((cols, cols), bf16),
            pltpu.VMEM((8, TILE, TILE), bf16),
            pltpu.VMEM((n, rows, cols), f32),
            pltpu.VMEM((n, rows, cols), f32),
            pltpu.VMEM((n, rows, cols), bf16),
            pltpu.VMEM((n, rows, cols), bf16),
            dma((6,)),
            dma((C + MOVED,)),
            dma((C + MOVED,)),
            dma((2 * C,)),
            dma((2 * C,)),
            dma((3 * C,)),
            dma((3 * C,)),
            dma((n, G)),
            dma((n, G)),
            dma((n, G)),
            dma((n, G)),
        ],
        compiler_params=pltpu.CompilerParams(
            collective_id=0, has_side_effects=True, vmem_limit_bytes=60 * 1024 * 1024),
    )(
        query_grads.reshape(rows, width),
        train_grads.reshape(cols, width),
        basis_out,
        basis_in,
        spectrum,
        train_ids,
    )


def solution(mesh):
    in_specs = (
        P(("parts", "blk"), "lay", None),
        P(("parts", "blk"), "lay", None),
        P("lay", None, None),
        P("lay", None, None),
        P("lay", None),
        P(("parts", "blk"), None),
    )
    out_specs = P(("parts", "lay"), "blk")
    n = mesh.shape["blk"]
    body = functools.partial(per_device, n) if n == mesh.shape["lay"] == 4 else plain
    return jax.shard_map(body, mesh=mesh, in_specs=in_specs, out_specs=out_specs, check_vma=False)
```

```python
import functools

import jax
import jax.numpy as jnp
from jax import lax
from jax.experimental import pallas as pl
from jax.experimental.pallas import tpu as pltpu
from jax.sharding import PartitionSpec as P

damping = 0.1
score_scale = 1.0 / 256.0
MESH = pl.DeviceIdType.MESH
f32 = jnp.float32
bf16 = jnp.bfloat16


def precondition(grads, basis_out, basis_in, spectrum):
    row_count = grads.shape[0]
    lay_count = grads.shape[1]
    out_dim = basis_out.shape[1]
    in_dim = basis_in.shape[1]
    field = grads.astype(jnp.float32).reshape(row_count, lay_count, out_dim, in_dim)
    high = lax.Precision.HIGHEST
    rotated = jnp.einsum("lap,mlab->mlpb", basis_out, field, precision=high)
    rotated = jnp.einsum("mlpb,lbr->mlpr", rotated, basis_in, precision=high)
    scaled = rotated / (spectrum.reshape(1, lay_count, out_dim, in_dim) + damping)
    restored = jnp.einsum("lap,mlpr->mlar", basis_out, scaled, precision=high)
    restored = jnp.einsum("mlar,lbr->mlab", restored, basis_in, precision=high)
    return restored.reshape(row_count, lay_count * out_dim * in_dim).astype(jnp.bfloat16)


def plain(query_grads, train_grads, basis_out, basis_in, spectrum, train_ids):
    prepared = precondition(query_grads, basis_out, basis_in, spectrum)
    local_rows = train_grads.reshape(train_grads.shape[0], -1)
    all_queries = lax.all_gather(prepared, "blk", axis=0, tiled=True)
    summed = lax.psum_scatter(
        lax.dot_general(
            all_queries, local_rows, (((1,), (1,)), ((), ())), preferred_element_type=jnp.float32
        ),
        "lay",
        scatter_dimension=0,
        tiled=True,
    )
    scaled_scores = summed * score_scale
    return jnp.take(scaled_scores, train_ids[0], axis=1)


def dot(a, b, dims=((1,), (0,))):
    return lax.dot_general(a, b, (dims, ((), ())), preferred_element_type=f32)


def split(x):
    hi = x.astype(bf16)
    return hi, (x - hi.astype(f32)).astype(bf16)


def dot3(a_hi, a_lo, b):
    b_hi, b_lo = split(b)
    return dot(a_hi, b_hi) + (dot(a_hi, b_lo) + dot(a_lo, b_hi))


CH = 16
GR = 64
SIDE = 64
TILE = 256
MOVED = 7


def kernel(n, q_hbm, t_hbm, bo_hbm, bi_hbm, sp_hbm, ids_hbm, o_ref,
           q_all, t_ref, bo_ref, bi_ref, sp_ref, ids_ref, sq_ref,
           x_ref, tp_hi, tp_lo, tp_end, perm, diag, stage, red, estage, ered,
           load_sem, a_send, a_recv, b_send, b_recv, c_send, c_recv,
           e_send, e_recv, r_send, r_recv):
    z = lax.axis_index("blk")
    l = lax.axis_index("lay")
    rows = q_hbm.shape[0]
    cols = t_ref.shape[0]
    width = q_hbm.shape[1]
    tiles = width // TILE
    C = rows // CH
    G = rows // GR
    KF = MOVED * TILE
    low = z < n // 2
    end = jnp.where(low, 0, n - 1)
    mid = jnp.where(low, 1, n - 2)
    far_mid = n - 1 - mid
    far_end = n - 1 - end
    at_end = z == end
    at_mid = z == mid

    def place(block, row, count, unit):
        return pl.ds(pl.multiple_of(block * rows + row, unit), count)

    loads = [
        pltpu.make_async_copy(q_hbm, q_all.at[place(z, 0, rows, rows), :], load_sem.at[0]),
        pltpu.make_async_copy(bo_hbm, bo_ref, load_sem.at[1]),
        pltpu.make_async_copy(bi_hbm, bi_ref, load_sem.at[2]),
        pltpu.make_async_copy(sp_hbm, sp_ref, load_sem.at[3]),
        pltpu.make_async_copy(ids_hbm, ids_ref, load_sem.at[4]),
        pltpu.make_async_copy(t_hbm, t_ref, load_sem.at[5]),
    ]
    for load in loads:
        load.start()

    barrier = pltpu.get_barrier_semaphore()
    partner = jnp.where(at_end, mid, end)
    for k in range(n):
        pl.semaphore_signal(
            barrier, inc=1, device_id={"blk": partner, "lay": k}, device_id_type=MESH)
    for k in range(1, n):
        pl.semaphore_signal(
            barrier, inc=1, device_id={"lay": lax.rem(l + k, n)}, device_id_type=MESH)

    @pl.when(at_mid)
    def _():
        pl.semaphore_signal(barrier, inc=1, device_id={"blk": far_mid}, device_id_type=MESH)

    def remote(src, dst, send, recv, target):
        return pltpu.make_async_remote_copy(
            src_ref=src, dst_ref=dst, send_sem=send, recv_sem=recv,
            device_id=target, device_id_type=MESH)

    def a_query(t):
        part = q_all.at[place(end, t * CH, CH, CH), :]
        return remote(part, part, a_send.at[t], a_recv.at[t], {"blk": mid})

    def a_train(m):
        piece = pl.ds(pl.multiple_of(m * TILE, TILE), TILE)
        return remote(tp_hi.at[piece, :], tp_end.at[piece, :],
                      a_send.at[C + m], a_recv.at[C + m], {"blk": mid})

    def b_out(t):
        part = q_all.at[place(jnp.where(t < C, mid, end), lax.rem(t, C) * CH, CH, CH), :]
        return remote(part, part, b_send.at[t], b_recv.at[t], {"blk": far_mid})

    def b_in(t):
        part = q_all.at[place(jnp.where(t < C, far_mid, far_end), lax.rem(t, C) * CH, CH, CH), :]
        return remote(part, part, b_send.at[t], b_recv.at[t], {"blk": far_mid})

    def c_own(t):
        part = q_all.at[place(mid, t * CH, CH, CH), pl.ds(KF, width - KF)]
        return remote(part, part, c_send.at[t], c_recv.at[t], {"blk": end})

    def c_far(t):
        part = q_all.at[place(jnp.where(t < C, far_mid, far_end), lax.rem(t, C) * CH, CH, CH),
                        pl.ds(KF, width - KF)]
        return remote(part, part, c_send.at[C + t], c_recv.at[C + t], {"blk": end})

    def e_copy(block, g, sender):
        part = pl.ds(pl.multiple_of(g * GR, GR), GR)
        return remote(estage.at[block, part, :], ered.at[sender, part, :],
                      e_send.at[block, g], e_recv.at[sender, g], {"blk": end, "lay": block})

    def r_copy(block, g, sender):
        part = pl.ds(pl.multiple_of(g * GR, GR), GR)
        return remote(stage.at[block, part, :], red.at[sender, part, :],
                      r_send.at[block, g], r_recv.at[sender, g], {"lay": block})

    for load in loads[1:5]:
        load.wait()
    row_i = lax.broadcasted_iota(jnp.int32, (TILE, SIDE), 0)
    col_i = lax.broadcasted_iota(jnp.int32, (TILE, SIDE), 1)
    pick = jnp.where(lax.rem(row_i, SIDE) == col_i, 1.0, 0.0).astype(bf16)
    big_r = lax.broadcasted_iota(jnp.int32, (TILE, TILE), 0)
    big_c = lax.broadcasted_iota(jnp.int32, (TILE, TILE), 1)
    same = big_r // SIDE == big_c // SIDE
    group = TILE // SIDE

    def spread(base, side):
        half = dot(pick, base, ((1,), (side,))).astype(bf16)
        full = dot(half, pick, ((1,), (1,)))
        return jnp.where(same, full, 0.0).astype(bf16)

    def prepare():
        for k, (ref, side) in enumerate(((bi_ref, 1), (bo_ref, 1), (bo_ref, 0), (bi_ref, 0))):
            hi, lo = split(ref[0])
            diag[2 * k] = spread(hi, side)
            diag[2 * k + 1] = spread(lo, side)
        perm[...] = jnp.where(big_r == ids_ref[...], 1.0, 0.0).astype(bf16)
        for p in range(SIDE):
            sq_ref[p:p + 1, :] = 1.0 / (sp_ref[:, p * SIDE:(p + 1) * SIDE] + damping)

    loads[0].wait()
    pl.semaphore_wait(barrier, 2 * n - 1 + at_mid.astype(jnp.int32))

    def scores(block, g, count, first=0):
        here = place(block, g * GR, count * GR, GR)
        part = q_all[here, first:]
        total = dot(part, tp_hi[first:, :]) + dot(part, tp_lo[first:, :])
        span = pl.ds(pl.multiple_of(g * GR, GR), count * GR)

        @pl.when(block == l)
        def _():
            red[l, span, :] = total

        @pl.when(block != l)
        def _():
            stage[block, span, :] = total
            for k in range(count):
                r_copy(block, g + k, l).start()

    def moved_scores(block, g, count):
        part = q_all[place(block, g * GR, count * GR, GR), :KF]
        span = pl.ds(pl.multiple_of(g * GR, GR), count * GR)
        estage[block, span, :] = dot(part, tp_end[...]).astype(bf16)
        for k in range(count):
            e_copy(block, g + k, l).start()

    def turn_in(i, carry):
        at = pl.multiple_of(i * TILE, TILE)
        x = dot(t_ref[:, pl.ds(at, TILE)], perm[...], ((0,), (0,))).astype(bf16)
        x = dot(diag[0], x) + dot(diag[1], x)
        for h in range(cols // 128):
            x_ref[h, pl.ds(at, TILE), :] = x[:, h * 128:(h + 1) * 128]
        return carry

    def turn_out(i, carry):
        halves = []
        for h in range(cols // 128):
            halves.append(jnp.concatenate(
                [x_ref[h, pl.ds(i * group + k, SIDE, stride=SIDE), :] for k in range(group)], axis=0))
        x = jnp.concatenate(halves, axis=1)
        x = dot3(diag[2], diag[3], x)
        lane = lax.broadcasted_iota(jnp.int32, (TILE, SIDE), 1)
        which = lax.broadcasted_iota(jnp.int32, (TILE, SIDE), 0) // SIDE + i * group
        values = jnp.concatenate([sq_ref[...]] * group, axis=0)
        x = x * jnp.sum(jnp.where(lane == which, values, 0.0), axis=1, keepdims=True)
        x = dot3(diag[4], diag[5], x)
        for h in range(cols // 128):
            for k in range(group):
                x_ref[h, pl.ds(i * group + k, SIDE, stride=SIDE), :] = (
                    x[k * SIDE:(k + 1) * SIDE, h * 128:(h + 1) * 128])
        return carry

    def turn_back(i, carry):
        at = pl.multiple_of(i * TILE, TILE)
        x = jnp.concatenate(
            [x_ref[h, pl.ds(at, TILE), :] for h in range(cols // 128)], axis=1)
        hi, lo = split(dot3(diag[6], diag[7], x))
        tp_hi[pl.ds(at, TILE), :] = hi
        tp_lo[pl.ds(at, TILE), :] = lo
        return carry

    LAG = 3
    D = 2

    def run(task, first, count):
        lax.fori_loop(0, count, lambda j, carry: task(first + j, carry), 0, unroll=4)

    PER = GR // CH

    def when(*parts):
        test = parts[0]
        for part in parts[1:]:
            test = test & part
        return pl.when(test)

    def within(t, first, last):
        return (t >= first) & (t < last)

    def step(t, carry):
        @when(at_end, within(t - LAG, 0, C))
        def _():
            a_query(t - LAG).wait_send()

        @when(at_end, within(t - LAG, C, C + MOVED))
        def _():
            a_train(t - LAG - C).wait_send()

        @when(at_end, t < C)
        def _():
            a_query(t).start()

        @when(at_end, within(t, C, C + MOVED))
        def _():
            a_train(t - C).start()

        @when(at_mid, within(t - LAG, 0, 2 * C))
        def _():
            b_out(t - LAG).wait_send()

        @when(at_mid, t < 2 * C)
        def _():
            b_out(t).start()

        even = lax.rem(t, 2) == 0

        @when(at_mid, even, t < 2 * C)
        def _():
            c_own(t // 2).start()

        @pl.when(t == 0)
        def _():
            prepare()
            loads[5].wait()

        @pl.when(t < 2)
        def _():
            run(turn_in, t * (tiles // 2), tiles // 2)

        @pl.when(within(t, 2, 6))
        def _():
            run(turn_out, (t - 2) * (tiles // 4), tiles // 4)

        @pl.when(within(t, 6, 8))
        def _():
            run(turn_back, (t - 6) * (tiles // 2), tiles // 2)

        r = t - D

        @when(at_mid, within(r, 0, C))
        def _():
            a_query(r).wait_recv()

        @when(at_mid, within(r, C, C + MOVED))
        def _():
            a_train(r - C).wait_recv()

        @when(at_mid, within(r, 0, 2 * C))
        def _():
            b_in(r).wait_recv()
            c_far(r).start()

        e = r - 1

        @when(at_end, within(e, 0, 2 * C), lax.rem(e, 2) == 0)
        def _():
            c_own(e // 2).wait_recv()

        @when(at_end, within(e, 0, 2 * C))
        def _():
            c_far(e).wait_recv()

        early = jnp.where(r == C - 1, mid, jnp.where(r == C, end, far_mid))

        @when(at_mid, within(r, C - 1, C + 2))
        def _():
            scores(early, 0, G)

        @when(at_mid, r == C + MOVED - 1)
        def _():
            moved_scores(mid, 0, G)
            moved_scores(far_mid, 0, G)
            moved_scores(far_end, 0, 1)

        @when(at_mid, r == 2 * C - 1)
        def _():
            moved_scores(far_end, 1, 1)

        @when(at_mid, within(r, C, 2 * C), lax.rem(r, PER) == PER - 1)
        def _():
            scores(far_end, lax.rem(r, C) // PER, 1)

        @when(at_end, e == C - 2)
        def _():
            scores(end, 0, G)

        @when(at_end, e == C)
        def _():
            scores(far_mid, 0, G, KF)

        @when(at_end, within(e, C, 2 * C), lax.rem(e, PER) == PER - 1)
        def _():
            scores(far_end, lax.rem(e, C) // PER, 1, KF)

        @when(at_end, e == 2 * C - 2)
        def _():
            scores(mid, 0, G, KF)
        return carry

    lax.fori_loop(0, 2 * C + LAG + 1, step, 0)

    @pl.when(at_mid)
    def _():
        def sent(t, carry):
            c_far(t).wait_send()
            return carry

        def sent_own(t, carry):
            c_own(t).wait_send()
            return carry

        lax.fori_loop(0, 2 * C, sent, 0)
        lax.fori_loop(0, C, sent_own, 0)
        for block in (mid, far_mid, far_end):
            for g in range(G):
                e_copy(block, g, l).wait_send()

    for k in range(1, n):
        other = lax.rem(l + k, n)
        for g in range(G):
            r_copy(other, g, l).wait_send()
            r_copy(other, g, other).wait_recv()
    total = red[0]
    for k in range(1, n):
        total = total + red[k]
    o_ref[...] = total * score_scale

    @pl.when(at_end & (l != end))
    def _():
        for k in range(n):
            for g in range(G):
                e_copy(l, g, k).wait_recv()
        extra = ered[0].astype(f32)
        for k in range(1, n):
            extra = extra + ered[k].astype(f32)
        o_ref[...] += extra * score_scale


def per_device(n, query_grads, train_grads, basis_out, basis_in, spectrum, train_ids):
    rows, lay_count, width = query_grads.shape
    cols = train_grads.shape[0]
    C = rows // CH
    G = rows // GR
    hbm = pl.BlockSpec(memory_space=pl.ANY)
    dma = pltpu.SemaphoreType.DMA
    return pl.pallas_call(
        functools.partial(kernel, n),
        out_shape=jax.ShapeDtypeStruct((rows, cols), f32),
        in_specs=[hbm] * 6,
        out_specs=pl.BlockSpec(memory_space=pltpu.VMEM),
        scratch_shapes=[
            pltpu.VMEM((n * rows, width), bf16),
            pltpu.VMEM((cols, width), bf16),
            pltpu.VMEM((1, SIDE, SIDE), f32),
            pltpu.VMEM((1, SIDE, SIDE), f32),
            pltpu.VMEM((1, width), f32),
            pltpu.VMEM((1, cols), jnp.int32),
            pltpu.VMEM((SIDE, SIDE), f32),
            pltpu.VMEM((cols // 128, width, 128), f32),
            pltpu.VMEM((width, cols), bf16),
            pltpu.VMEM((width, cols), bf16),
            pltpu.VMEM((MOVED * TILE, cols), bf16),
            pltpu.VMEM((cols, cols), bf16),
            pltpu.VMEM((8, TILE, TILE), bf16),
            pltpu.VMEM((n, rows, cols), f32),
            pltpu.VMEM((n, rows, cols), f32),
            pltpu.VMEM((n, rows, cols), bf16),
            pltpu.VMEM((n, rows, cols), bf16),
            dma((6,)),
            dma((C + MOVED,)),
            dma((C + MOVED,)),
            dma((2 * C,)),
            dma((2 * C,)),
            dma((3 * C,)),
            dma((3 * C,)),
            dma((n, G)),
            dma((n, G)),
            dma((n, G)),
            dma((n, G)),
        ],
        compiler_params=pltpu.CompilerParams(
            collective_id=0, has_side_effects=True, vmem_limit_bytes=60 * 1024 * 1024),
    )(
        query_grads.reshape(rows, width),
        train_grads.reshape(cols, width),
        basis_out,
        basis_in,
        spectrum,
        train_ids,
    )


def solution(mesh):
    in_specs = (
        P(("parts", "blk"), "lay", None),
        P(("parts", "blk"), "lay", None),
        P("lay", None, None),
        P("lay", None, None),
        P("lay", None),
        P(("parts", "blk"), None),
    )
    out_specs = P(("parts", "lay"), "blk")
    n = mesh.shape["blk"]
    body = functools.partial(per_device, n) if n == mesh.shape["lay"] == 4 else plain
    return jax.shard_map(body, mesh=mesh, in_specs=in_specs, out_specs=out_specs, check_vma=False)
```

```python
import functools

import jax
import jax.numpy as jnp
from jax import lax
from jax.experimental import pallas as pl
from jax.experimental.pallas import tpu as pltpu
from jax.sharding import PartitionSpec as P

damping = 0.1
score_scale = 1.0 / 256.0
MESH = pl.DeviceIdType.MESH
f32 = jnp.float32
bf16 = jnp.bfloat16


def precondition(grads, basis_out, basis_in, spectrum):
    row_count = grads.shape[0]
    lay_count = grads.shape[1]
    out_dim = basis_out.shape[1]
    in_dim = basis_in.shape[1]
    field = grads.astype(jnp.float32).reshape(row_count, lay_count, out_dim, in_dim)
    high = lax.Precision.HIGHEST
    rotated = jnp.einsum("lap,mlab->mlpb", basis_out, field, precision=high)
    rotated = jnp.einsum("mlpb,lbr->mlpr", rotated, basis_in, precision=high)
    scaled = rotated / (spectrum.reshape(1, lay_count, out_dim, in_dim) + damping)
    restored = jnp.einsum("lap,mlpr->mlar", basis_out, scaled, precision=high)
    restored = jnp.einsum("mlar,lbr->mlab", restored, basis_in, precision=high)
    return restored.reshape(row_count, lay_count * out_dim * in_dim).astype(jnp.bfloat16)


def plain(query_grads, train_grads, basis_out, basis_in, spectrum, train_ids):
    prepared = precondition(query_grads, basis_out, basis_in, spectrum)
    local_rows = train_grads.reshape(train_grads.shape[0], -1)
    all_queries = lax.all_gather(prepared, "blk", axis=0, tiled=True)
    summed = lax.psum_scatter(
        lax.dot_general(
            all_queries, local_rows, (((1,), (1,)), ((), ())), preferred_element_type=jnp.float32
        ),
        "lay",
        scatter_dimension=0,
        tiled=True,
    )
    scaled_scores = summed * score_scale
    return jnp.take(scaled_scores, train_ids[0], axis=1)


def dot(a, b, dims=((1,), (0,))):
    return lax.dot_general(a, b, (dims, ((), ())), preferred_element_type=f32)


def split(x):
    hi = x.astype(bf16)
    return hi, (x - hi.astype(f32)).astype(bf16)


def dot3(a_hi, a_lo, b):
    b_hi, b_lo = split(b)
    return dot(a_hi, b_hi) + (dot(a_hi, b_lo) + dot(a_lo, b_hi))


CH = 16
GR = 64
SIDE = 64
TILE = 256
MOVED = 7


def kernel(n, q_hbm, t_hbm, bo_hbm, bi_hbm, sp_hbm, ids_hbm, o_ref,
           q_all, t_ref, bo_ref, bi_ref, sp_ref, ids_ref, sq_ref,
           x_ref, tp_hi, tp_end, perm, diag, stage, red, estage, ered,
           load_sem, a_send, a_recv, b_send, b_recv, c_send, c_recv,
           e_send, e_recv, r_send, r_recv):
    z = lax.axis_index("blk")
    l = lax.axis_index("lay")
    rows = q_hbm.shape[0]
    cols = t_ref.shape[0]
    width = q_hbm.shape[1]
    tiles = width // TILE
    C = rows // CH
    G = rows // GR
    KF = MOVED * TILE
    low = z < n // 2
    end = jnp.where(low, 0, n - 1)
    mid = jnp.where(low, 1, n - 2)
    far_mid = n - 1 - mid
    far_end = n - 1 - end
    at_end = z == end
    at_mid = z == mid

    def place(block, row, count, unit):
        return pl.ds(pl.multiple_of(block * rows + row, unit), count)

    loads = [
        pltpu.make_async_copy(q_hbm, q_all.at[place(z, 0, rows, rows), :], load_sem.at[0]),
        pltpu.make_async_copy(bo_hbm, bo_ref, load_sem.at[1]),
        pltpu.make_async_copy(bi_hbm, bi_ref, load_sem.at[2]),
        pltpu.make_async_copy(sp_hbm, sp_ref, load_sem.at[3]),
        pltpu.make_async_copy(ids_hbm, ids_ref, load_sem.at[4]),
        pltpu.make_async_copy(t_hbm, t_ref, load_sem.at[5]),
    ]
    for load in loads:
        load.start()

    barrier = pltpu.get_barrier_semaphore()
    partner = jnp.where(at_end, mid, end)
    for k in range(n):
        pl.semaphore_signal(
            barrier, inc=1, device_id={"blk": partner, "lay": k}, device_id_type=MESH)
    for k in range(1, n):
        pl.semaphore_signal(
            barrier, inc=1, device_id={"lay": lax.rem(l + k, n)}, device_id_type=MESH)

    @pl.when(at_mid)
    def _():
        pl.semaphore_signal(barrier, inc=1, device_id={"blk": far_mid}, device_id_type=MESH)

    def remote(src, dst, send, recv, target):
        return pltpu.make_async_remote_copy(
            src_ref=src, dst_ref=dst, send_sem=send, recv_sem=recv,
            device_id=target, device_id_type=MESH)

    def a_query(t):
        part = q_all.at[place(end, t * CH, CH, CH), :]
        return remote(part, part, a_send.at[t], a_recv.at[t], {"blk": mid})

    def a_train(m):
        piece = pl.ds(pl.multiple_of(m * TILE, TILE), TILE)
        return remote(tp_hi.at[piece, :], tp_end.at[piece, :],
                      a_send.at[C + m], a_recv.at[C + m], {"blk": mid})

    def b_out(t):
        part = q_all.at[place(jnp.where(t < C, mid, end), lax.rem(t, C) * CH, CH, CH), :]
        return remote(part, part, b_send.at[t], b_recv.at[t], {"blk": far_mid})

    def b_in(t):
        part = q_all.at[place(jnp.where(t < C, far_mid, far_end), lax.rem(t, C) * CH, CH, CH), :]
        return remote(part, part, b_send.at[t], b_recv.at[t], {"blk": far_mid})

    def c_own(t):
        part = q_all.at[place(mid, t * CH, CH, CH), pl.ds(KF, width - KF)]
        return remote(part, part, c_send.at[t], c_recv.at[t], {"blk": end})

    def c_far(t):
        part = q_all.at[place(jnp.where(t < C, far_mid, far_end), lax.rem(t, C) * CH, CH, CH),
                        pl.ds(KF, width - KF)]
        return remote(part, part, c_send.at[C + t], c_recv.at[C + t], {"blk": end})

    def e_copy(block, g, sender):
        part = pl.ds(pl.multiple_of(g * GR, GR), GR)
        return remote(estage.at[block, part, :], ered.at[sender, part, :],
                      e_send.at[block, g], e_recv.at[sender, g], {"blk": end, "lay": block})

    def r_copy(block, g, sender):
        part = pl.ds(pl.multiple_of(g * GR, GR), GR)
        return remote(stage.at[block, part, :], red.at[sender, part, :],
                      r_send.at[block, g], r_recv.at[sender, g], {"lay": block})

    for load in loads[1:5]:
        load.wait()
    row_i = lax.broadcasted_iota(jnp.int32, (TILE, SIDE), 0)
    col_i = lax.broadcasted_iota(jnp.int32, (TILE, SIDE), 1)
    pick = jnp.where(lax.rem(row_i, SIDE) == col_i, 1.0, 0.0).astype(bf16)
    big_r = lax.broadcasted_iota(jnp.int32, (TILE, TILE), 0)
    big_c = lax.broadcasted_iota(jnp.int32, (TILE, TILE), 1)
    same = big_r // SIDE == big_c // SIDE
    group = TILE // SIDE

    def spread(base, side):
        half = dot(pick, base, ((1,), (side,))).astype(bf16)
        full = dot(half, pick, ((1,), (1,)))
        return jnp.where(same, full, 0.0).astype(bf16)

    def prepare():
        for k, (ref, side) in enumerate(((bi_ref, 1), (bo_ref, 1), (bo_ref, 0), (bi_ref, 0))):
            hi, lo = split(ref[0])
            diag[2 * k] = spread(hi, side)
            diag[2 * k + 1] = spread(lo, side)
        perm[...] = jnp.where(big_r == ids_ref[...], 1.0, 0.0).astype(bf16)
        for p in range(SIDE):
            sq_ref[p:p + 1, :] = 1.0 / (sp_ref[:, p * SIDE:(p + 1) * SIDE] + damping)

    loads[0].wait()
    pl.semaphore_wait(barrier, 2 * n - 1 + at_mid.astype(jnp.int32))

    def scores(block, g, count, first=0):
        here = place(block, g * GR, count * GR, GR)
        part = q_all[here, first:]
        total = dot(part, tp_hi[first:, :])
        span = pl.ds(pl.multiple_of(g * GR, GR), count * GR)

        @pl.when(block == l)
        def _():
            red[l, span, :] = total

        @pl.when(block != l)
        def _():
            stage[block, span, :] = total
            for k in range(count):
                r_copy(block, g + k, l).start()

    def moved_scores(block, g, count):
        part = q_all[place(block, g * GR, count * GR, GR), :KF]
        span = pl.ds(pl.multiple_of(g * GR, GR), count * GR)
        estage[block, span, :] = dot(part, tp_end[...]).astype(bf16)
        for k in range(count):
            e_copy(block, g + k, l).start()

    def turn_in(i, carry):
        at = pl.multiple_of(i * TILE, TILE)
        x = dot(t_ref[:, pl.ds(at, TILE)], perm[...], ((0,), (0,))).astype(bf16)
        x = dot(diag[0], x) + dot(diag[1], x)
        for h in range(cols // 128):
            x_ref[h, pl.ds(at, TILE), :] = x[:, h * 128:(h + 1) * 128]
        return carry

    def turn_out(i, carry):
        halves = []
        for h in range(cols // 128):
            halves.append(jnp.concatenate(
                [x_ref[h, pl.ds(i * group + k, SIDE, stride=SIDE), :] for k in range(group)], axis=0))
        x = jnp.concatenate(halves, axis=1)
        x = dot3(diag[2], diag[3], x)
        lane = lax.broadcasted_iota(jnp.int32, (TILE, SIDE), 1)
        which = lax.broadcasted_iota(jnp.int32, (TILE, SIDE), 0) // SIDE + i * group
        values = jnp.concatenate([sq_ref[...]] * group, axis=0)
        x = x * jnp.sum(jnp.where(lane == which, values, 0.0), axis=1, keepdims=True)
        x = dot3(diag[4], diag[5], x)
        for h in range(cols // 128):
            for k in range(group):
                x_ref[h, pl.ds(i * group + k, SIDE, stride=SIDE), :] = (
                    x[k * SIDE:(k + 1) * SIDE, h * 128:(h + 1) * 128])
        return carry

    def turn_back(i, carry):
        at = pl.multiple_of(i * TILE, TILE)
        x = jnp.concatenate(
            [x_ref[h, pl.ds(at, TILE), :] for h in range(cols // 128)], axis=1)
        tp_hi[pl.ds(at, TILE), :] = dot3(diag[6], diag[7], x).astype(bf16)
        return carry

    LAG = 3
    D = 2

    def run(task, first, count):
        lax.fori_loop(0, count, lambda j, carry: task(first + j, carry), 0, unroll=4)

    PER = GR // CH

    def when(*parts):
        test = parts[0]
        for part in parts[1:]:
            test = test & part
        return pl.when(test)

    def within(t, first, last):
        return (t >= first) & (t < last)

    def step(t, carry):
        @when(at_end, within(t - LAG, 0, C))
        def _():
            a_query(t - LAG).wait_send()

        @when(at_end, within(t - LAG, C, C + MOVED))
        def _():
            a_train(t - LAG - C).wait_send()

        @when(at_end, t < C)
        def _():
            a_query(t).start()

        @when(at_end, within(t, C, C + MOVED))
        def _():
            a_train(t - C).start()

        @when(at_mid, within(t - LAG, 0, 2 * C))
        def _():
            b_out(t - LAG).wait_send()

        @when(at_mid, t < 2 * C)
        def _():
            b_out(t).start()

        even = lax.rem(t, 2) == 0

        @when(at_mid, even, t < 2 * C)
        def _():
            c_own(t // 2).start()

        @pl.when(t == 0)
        def _():
            prepare()
            loads[5].wait()

        @pl.when(t < 2)
        def _():
            run(turn_in, t * (tiles // 2), tiles // 2)

        @pl.when(within(t, 2, 6))
        def _():
            run(turn_out, (t - 2) * (tiles // 4), tiles // 4)

        @pl.when(within(t, 6, 8))
        def _():
            run(turn_back, (t - 6) * (tiles // 2), tiles // 2)

        r = t - D

        @when(at_mid, within(r, 0, C))
        def _():
            a_query(r).wait_recv()

        @when(at_mid, within(r, C, C + MOVED))
        def _():
            a_train(r - C).wait_recv()

        @when(at_mid, within(r, 0, 2 * C))
        def _():
            b_in(r).wait_recv()
            c_far(r).start()

        e = r - 1

        @when(at_end, within(e, 0, 2 * C), lax.rem(e, 2) == 0)
        def _():
            c_own(e // 2).wait_recv()

        @when(at_end, within(e, 0, 2 * C))
        def _():
            c_far(e).wait_recv()

        early = jnp.where(r == C - 1, mid, jnp.where(r == C, end, far_mid))

        @when(at_mid, within(r, C - 1, C + 2))
        def _():
            scores(early, 0, G)

        @when(at_mid, r == C + MOVED - 1)
        def _():
            moved_scores(mid, 0, G)
            moved_scores(far_mid, 0, G)
            moved_scores(far_end, 0, 1)

        @when(at_mid, r == 2 * C - 1)
        def _():
            moved_scores(far_end, 1, 1)

        @when(at_mid, within(r, C, 2 * C), lax.rem(r, PER) == PER - 1)
        def _():
            scores(far_end, lax.rem(r, C) // PER, 1)

        @when(at_end, e == C - 2)
        def _():
            scores(end, 0, G)

        @when(at_end, e == C)
        def _():
            scores(far_mid, 0, G, KF)

        @when(at_end, within(e, C, 2 * C), lax.rem(e, PER) == PER - 1)
        def _():
            scores(far_end, lax.rem(e, C) // PER, 1, KF)

        @when(at_end, e == 2 * C - 2)
        def _():
            scores(mid, 0, G, KF)
        return carry

    lax.fori_loop(0, 2 * C + LAG + 1, step, 0)

    @pl.when(at_mid)
    def _():
        def sent(t, carry):
            c_far(t).wait_send()
            return carry

        def sent_own(t, carry):
            c_own(t).wait_send()
            return carry

        lax.fori_loop(0, 2 * C, sent, 0)
        lax.fori_loop(0, C, sent_own, 0)
        for block in (mid, far_mid, far_end):
            for g in range(G):
                e_copy(block, g, l).wait_send()

    for k in range(1, n):
        other = lax.rem(l + k, n)
        for g in range(G):
            r_copy(other, g, l).wait_send()
            r_copy(other, g, other).wait_recv()
    total = red[0]
    for k in range(1, n):
        total = total + red[k]
    o_ref[...] = total * score_scale

    @pl.when(at_end & (l != end))
    def _():
        for k in range(n):
            for g in range(G):
                e_copy(l, g, k).wait_recv()
        extra = ered[0].astype(f32)
        for k in range(1, n):
            extra = extra + ered[k].astype(f32)
        o_ref[...] += extra * score_scale


def per_device(n, query_grads, train_grads, basis_out, basis_in, spectrum, train_ids):
    rows, lay_count, width = query_grads.shape
    cols = train_grads.shape[0]
    C = rows // CH
    G = rows // GR
    hbm = pl.BlockSpec(memory_space=pl.ANY)
    dma = pltpu.SemaphoreType.DMA
    return pl.pallas_call(
        functools.partial(kernel, n),
        out_shape=jax.ShapeDtypeStruct((rows, cols), f32),
        in_specs=[hbm] * 6,
        out_specs=pl.BlockSpec(memory_space=pltpu.VMEM),
        scratch_shapes=[
            pltpu.VMEM((n * rows, width), bf16),
            pltpu.VMEM((cols, width), bf16),
            pltpu.VMEM((1, SIDE, SIDE), f32),
            pltpu.VMEM((1, SIDE, SIDE), f32),
            pltpu.VMEM((1, width), f32),
            pltpu.VMEM((1, cols), jnp.int32),
            pltpu.VMEM((SIDE, SIDE), f32),
            pltpu.VMEM((cols // 128, width, 128), f32),
            pltpu.VMEM((width, cols), bf16),
            pltpu.VMEM((MOVED * TILE, cols), bf16),
            pltpu.VMEM((cols, cols), bf16),
            pltpu.VMEM((8, TILE, TILE), bf16),
            pltpu.VMEM((n, rows, cols), f32),
            pltpu.VMEM((n, rows, cols), f32),
            pltpu.VMEM((n, rows, cols), bf16),
            pltpu.VMEM((n, rows, cols), bf16),
            dma((6,)),
            dma((C + MOVED,)),
            dma((C + MOVED,)),
            dma((2 * C,)),
            dma((2 * C,)),
            dma((3 * C,)),
            dma((3 * C,)),
            dma((n, G)),
            dma((n, G)),
            dma((n, G)),
            dma((n, G)),
        ],
        compiler_params=pltpu.CompilerParams(
            collective_id=0, has_side_effects=True, vmem_limit_bytes=60 * 1024 * 1024),
    )(
        query_grads.reshape(rows, width),
        train_grads.reshape(cols, width),
        basis_out,
        basis_in,
        spectrum,
        train_ids,
    )


def solution(mesh):
    in_specs = (
        P(("parts", "blk"), "lay", None),
        P(("parts", "blk"), "lay", None),
        P("lay", None, None),
        P("lay", None, None),
        P("lay", None),
        P(("parts", "blk"), None),
    )
    out_specs = P(("parts", "lay"), "blk")
    n = mesh.shape["blk"]
    body = functools.partial(per_device, n) if n == mesh.shape["lay"] == 4 else plain
    return jax.shard_map(body, mesh=mesh, in_specs=in_specs, out_specs=out_specs, check_vma=False)
```
